128 devices in a mesh: dp: 32 (over x, y, z_hi), narrow: 4 (over z_lo, core).
Axes of the slice: x: 4, y: 4, z: 4 (z_hi: 2, z_lo: 2; z = z_hi * 2 + z_lo), core: 2. Of those that a mesh axis runs over, the one named last changes fastest.
Arguments:
- picture_features: bfloat16 [98304, 1152], P(('dp', 'narrow')), may hold values from -1.0234375 to 1.0234375
- caption_features: bfloat16 [98304, 1152], P(('dp', 'narrow')), may hold values from -1.0234375 to 1.0234375
- match_identifiers: int32 [98304], replicated, may hold values from 0 to 767
- trading_step_number: int32 [1], replicated, may hold values from 1 to 31
- sharpness_coefficient: float32 [1], replicated, may hold values from 0.5 to 2
- offset_term: float32 [1], replicated, may hold values from -2 to 0
Outputs:
- grad_image: float32 [98304, 1152], P(('dp', 'narrow'))
- text_embedding_gradient: float32 [98304, 1152], P(('dp', 'narrow'))
- row_loss: float32 [98304], P(('dp', 'narrow'))
The draws below stay inside these ranges and needn't reach their ends.
All inputs are finite; a program needn't handle non-finite values.
Results may differ from the reference program's by a relative error of at most 0.0034.
Values may be sent and summed in bfloat16 or wider, within the bound.
No kernel may reach another device: no remote copies, remote signals or barrier semaphores. Data moves between devices by JAX's collectives and lax.ppermute only.
A program may use at most 128 MiB of HBM per device.

```python
import math
import jax
import jax.numpy as jnp
from jax import lax

D = 1152
B_DEV = 768
ROWS = 98304
N_DP = 32
N_NARROW = 4


def plant(result, own_key, low, largest):
    spot = [jax.random.randint(jax.random.fold_in(own_key, axis), (), 0, length) for axis, length in enumerate(result.shape)]
    main_axis = result.shape.index(max(result.shape))
    beside = spot[:main_axis] + [(spot[main_axis] + 1) % result.shape[main_axis]] + spot[main_axis + 1:]
    return result.at[tuple(spot)].set(low).at[tuple(beside)].set(largest)


def level_of(stream_key, shape, shards, low, largest):
    level = 1.0
    for axis_at, blocks in shards:
        heights = jax.random.uniform(jax.random.fold_in(jax.random.fold_in(stream_key, 6), axis_at), (blocks,), jnp.float32, low / len(shards), largest / len(shards))
        level = level * jnp.repeat(jnp.exp(heights), shape[axis_at] // blocks).reshape((-1,) + (1,) * (len(shape) - 1 - axis_at))
    return level


def noise(key, shape, spread, reach, pieces=(), kind=jnp.bfloat16):
    entries = jax.random.normal(key, shape, jnp.float32) * spread
    if len(pieces) > 0:
        entries = level_of(key, shape, pieces, -0.22, 0.18) * entries
    return jnp.clip(entries, min=-reach, max=reach).astype(kind)


def setup_inputs(seed: int = 0) -> dict:
    seeds = jax.random.split(jax.random.key(seed), 7)
    return {
        "picture_features": noise(seeds[0], (ROWS, D), (1.0 / D ** 0.25), 1.0234375, ((0, 128),)),
        "caption_features": noise(seeds[1], (ROWS, D), (1.0 / D ** 0.25), 1.0234375, ((0, 128),)),
        "match_identifiers": plant(jax.random.randint(seeds[2], (ROWS,), 0, B_DEV * N_NARROW // 4), jax.random.fold_in(seeds[2], 1), 0, (B_DEV * N_NARROW // 4) - 1).astype(jnp.int32),
        "trading_step_number": jax.random.randint(seeds[3], (1,), 1, N_DP).astype(jnp.int32),
        "sharpness_coefficient": jnp.clip(jnp.exp(jax.random.uniform(seeds[4], (1,), jnp.float32, math.log(0.5), math.log(2.0))), 0.5, 2.0),
        "offset_term": jnp.clip(jax.random.uniform(seeds[5], (1,), jnp.float32, -2.0, 0.0), -2.0, 0.0),
    }


def reference(picture_features, caption_features, match_identifiers, trading_step_number, sharpness_coefficient, offset_term):
    group_rows = B_DEV * N_NARROW
    rnd = trading_step_number[0]
    multiplier_value = sharpness_coefficient[0]
    shift = offset_term[0]
    images = picture_features.reshape(N_DP, group_rows, D)
    texts = caption_features.reshape(N_DP, group_rows, D)
    labels = match_identifiers.reshape(N_DP, group_rows)

    def one_group(group):
        partner = jnp.bitwise_xor(group, rnd)
        left = images[group]
        right = texts[partner]
        logits = multiplier_value * jnp.dot(left, right.T, preferred_element_type=jnp.float32) + shift
        same = labels[group][:, None] == labels[partner][None, :]
        sign = jnp.where(same, 1.0, -1.0).astype(jnp.float32)
        pair_loss = -jax.nn.log_sigmoid(sign * logits)
        coef = (-sign * jax.nn.sigmoid(-sign * logits)).astype(jnp.bfloat16)
        grad_left = multiplier_value * jnp.dot(coef, right, preferred_element_type=jnp.float32)
        text_part = (multiplier_value * jnp.dot(coef.T, left, preferred_element_type=jnp.float32)).astype(jnp.bfloat16)
        return grad_left, text_part, jnp.mean(pair_loss, axis=1)

    grad_left, text_part, losses = lax.map(one_group, jnp.arange(N_DP, dtype=jnp.int32))
    order = jnp.bitwise_xor(jnp.arange(N_DP, dtype=jnp.int32), rnd)
    text_embedding_gradient = text_part[order].astype(jnp.float32).reshape(N_DP * group_rows, D)
    return grad_left.reshape(N_DP * group_rows, D), text_embedding_gradient, losses.reshape(N_DP * group_rows)
```

```python
import jax
import jax.numpy as jnp
from jax import lax
from jax.sharding import PartitionSpec as P

AXES = ("dp", "narrow")


def xor_route(count, mask):
    return [(d, d ^ mask) for d in range(count)]


def pair_terms(logits, left_ids, right_ids):
    same = left_ids[:, None] == right_ids[None, :]
    z = jnp.where(same, logits, -logits)
    tail = jnp.exp(-jnp.abs(z))
    pair_loss = jnp.maximum(-z, 0.0) + jnp.log1p(tail)
    share = jnp.where(z > 0, tail, 1.0) / (1.0 + tail)
    coef = jnp.where(same, -share, share).astype(jnp.bfloat16)
    return pair_loss, coef


def dot(a, b, dims):
    return lax.dot_general(a, b, (dims, ((), ())), preferred_element_type=jnp.float32)


def exchange_round(rnd, count, width, picture, caption, ids, scale, shift):
    rows = picture.shape[0]
    half = width // 2
    flip = half if rnd & 1 else 0
    route = xor_route(count, (rnd * width) | flip)
    over_z = xor_route(count, half)
    over_core = xor_route(count, 1)
    me = lax.axis_index("dp") * width + lax.axis_index("narrow")

    text_own = lax.ppermute(caption, AXES, route)
    image_far = lax.ppermute(picture, AXES, over_z)
    text_near = lax.ppermute(text_own, AXES, over_core)

    text_at = me ^ ((rnd * width) | flip)
    take = lambda device: lax.dynamic_slice_in_dim(ids, device * rows, rows)
    image_ids = jnp.concatenate([take(me), take(me ^ half)])
    text_ids = jnp.concatenate([take(text_at), take(text_at ^ 1)])
    images = jnp.concatenate([picture, image_far])
    texts = jnp.concatenate([text_own, text_near])

    logits = scale * dot(images, texts, ((1,), (1,))) + shift
    pair_loss, coef = pair_terms(logits, image_ids, text_ids)
    loss_sum = jnp.sum(pair_loss, axis=1)

    text_far_part = scale * dot(coef[:, rows:], images, ((0,), (0,)))
    text_far_part = lax.ppermute(text_far_part, AXES, over_core)
    text_part = scale * dot(coef[:, :rows], images, ((0,), (0,)))
    text_part = (text_part + text_far_part).astype(jnp.bfloat16)
    text_grad = lax.ppermute(text_part, AXES, route).astype(jnp.float32)

    image_far_part = (scale * dot(coef[rows:], texts, ((1,), (0,)))).astype(jnp.bfloat16)
    image_far_part = lax.ppermute(image_far_part, AXES, over_z)
    loss_far = lax.ppermute(loss_sum[rows:], AXES, over_z)
    image_grad = scale * dot(coef[:rows], texts, ((1,), (0,))) + image_far_part.astype(jnp.float32)
    row_loss = (loss_sum[:rows] + loss_far) / (rows * width)
    return image_grad, text_grad, row_loss


def solution(mesh):
    groups, width = mesh.shape["dp"], mesh.shape["narrow"]
    count = groups * width

    def per_device(picture, caption, ids, rnd, scale, shift):
        branches = [
            lambda *args, r=r: exchange_round(r, count, width, *args) for r in range(1, groups)
        ]
        return lax.switch(rnd[0] - 1, branches, picture, caption, ids, scale[0], shift[0])

    in_specs = (P(AXES, None), P(AXES, None), P(), P(), P(), P())
    out_specs = (P(AXES, None), P(AXES, None), P(AXES))
    return jax.shard_map(
        per_device, mesh=mesh, in_specs=in_specs, out_specs=out_specs, check_vma=False
    )
```

```python
import jax
import jax.numpy as jnp
from jax import lax
from jax.sharding import PartitionSpec as P

AXES = ("dp", "narrow")


def xor_route(count, mask):
    return [(d, d ^ mask) for d in range(count)]


def pair_terms(logits, left_ids, right_ids):
    same = left_ids[:, None] == right_ids[None, :]
    z = jnp.where(same, logits, -logits)
    tail = jnp.exp(-jnp.abs(z))
    pair_loss = jnp.maximum(-z, 0.0) + jnp.log1p(tail)
    share = jnp.where(z > 0, tail, 1.0) / (1.0 + tail)
    coef = jnp.where(same, -share, share).astype(jnp.bfloat16)
    return pair_loss, coef


def dot(a, b, dims):
    return lax.dot_general(a, b, (dims, ((), ())), preferred_element_type=jnp.float32)


def partner_mask(rnd, width):
    return rnd * width ^ (rnd & 1) * (width // 2)


def solution(mesh):
    groups, width = mesh.shape["dp"], mesh.shape["narrow"]
    count, half = groups * width, width // 2
    over_z = xor_route(count, half)
    over_core = xor_route(count, 1)

    def forward(rnd, caption, picture):
        text_own = lax.ppermute(caption, AXES, xor_route(count, partner_mask(rnd, width)))
        image_far = lax.ppermute(picture, AXES, over_z)
        return text_own, image_far

    def backward(rnd, text_part, image_far_part, loss_far):
        loss_far = lax.ppermute(loss_far, AXES, over_z)
        text_grad = lax.ppermute(text_part, AXES, xor_route(count, partner_mask(rnd, width)))
        image_far_part = lax.ppermute(image_far_part, AXES, over_z)
        return text_grad, image_far_part, loss_far

    def by_round(step, which, *args):
        branches = [lambda *a, r=r: step(r, *a) for r in range(1, groups)]
        return lax.switch(which, branches, *args)

    def per_device(picture, caption, ids, rnd, scale, shift):
        rnd, scale, shift = rnd[0], scale[0], shift[0]
        rows = picture.shape[0]
        me = lax.axis_index("dp") * width + lax.axis_index("narrow")
        text_at = me ^ partner_mask(rnd, width)
        take = lambda device: lax.dynamic_slice_in_dim(ids, device * rows, rows)
        image_ids = jnp.concatenate([take(me), take(me ^ half)])
        text_ids = jnp.concatenate([take(text_at), take(text_at ^ 1)])

        text_own, image_far = by_round(forward, rnd - 1, caption, picture)
        text_near = lax.ppermute(text_own, AXES, over_core)
        images = jnp.concatenate([picture, image_far])
        texts = jnp.concatenate([text_own, text_near])

        logits = scale * dot(images, texts, ((1,), (1,))) + shift
        pair_loss, coef = pair_terms(logits, image_ids, text_ids)
        loss_sum = jnp.sum(pair_loss, axis=1)

        text_far_part = scale * dot(coef[:, rows:], images, ((0,), (0,)))
        text_far_part = lax.ppermute(text_far_part, AXES, over_core)
        text_part = scale * dot(coef[:, :rows], images, ((0,), (0,)))
        text_part = (text_part + text_far_part).astype(jnp.bfloat16)
        image_far_part = (scale * dot(coef[rows:], texts, ((1,), (0,)))).astype(jnp.bfloat16)
        image_grad = scale * dot(coef[:rows], texts, ((1,), (0,)))

        text_grad, image_far_part, loss_far = by_round(
            backward, rnd - 1, text_part, image_far_part, loss_sum[rows:]
        )
        image_grad = image_grad + image_far_part.astype(jnp.float32)
        row_loss = (loss_sum[:rows] + loss_far) / (rows * width)
        return image_grad, text_grad.astype(jnp.float32), row_loss

    in_specs = (P(AXES, None), P(AXES, None), P(), P(), P(), P())
    out_specs = (P(AXES, None), P(AXES, None), P(AXES))
    return jax.shard_map(
        per_device, mesh=mesh, in_specs=in_specs, out_specs=out_specs, check_vma=False
    )
```

```python
import math

import jax
import jax.numpy as jnp
from jax import lax
from jax.experimental import pallas as pl
from jax.experimental.pallas import tpu as pltpu
from jax.sharding import PartitionSpec as P

AXES = ("dp", "narrow")
BLOCK = 256
CHUNK = 16
LOG2E = 1.0 / math.log(2.0)


def dot(a, b, dims):
    return lax.dot_general(a, b, (dims, ((), ())), preferred_element_type=jnp.float32)


def log1p(q):
    small = q * (1.0 - q * (0.5 - q * (1.0 / 3.0 - q * 0.25)))
    return jnp.where(q < 0.01, small, jnp.log(1.0 + q))


def pair_body(first, steps, text_rows, *refs):
    if first:
        (params, image_ids, text_ids, near, far, text, image_out, loss_out, text_out,
         coef, ids_column) = refs
    else:
        (params, image_ids, text_ids, near, far, text, image_in, loss_in,
         own_out, far_out, loss_out, text_out, coef, ids_column) = refs
    step = pl.program_id(0)
    scale = params[0]

    @pl.when(step == 0)
    def _():
        for k in range(text_rows // 128):
            part = jnp.broadcast_to(text_ids[:, k * 128 : (k + 1) * 128], (128, 128))
            ids_column[k * 128 : (k + 1) * 128, :] = part.T

    @pl.when(step < steps)
    def _():
        half = steps // 2
        row = pl.multiple_of(lax.rem(step, half) * BLOCK, BLOCK)
        is_near = step < half
        images = jnp.where(is_near, near[pl.ds(row, BLOCK), :], far[pl.ds(row, BLOCK), :])
        raw = dot(text[...], images, ((1,), (1,)))
        left = jnp.broadcast_to(image_ids[...], (CHUNK, BLOCK))
        gain, shift = scale * LOG2E, params[1] * LOG2E
        linear = jnp.zeros((CHUNK, BLOCK), jnp.float32)
        product = jnp.zeros((CHUNK, BLOCK), jnp.float32)
        column = pl.multiple_of(step * BLOCK, BLOCK)
        for at in range(0, text_rows, CHUNK):
            logit = raw[at : at + CHUNK] * gain + shift
            right = ids_column[at : at + CHUNK, :]
            same = left == jnp.concatenate([right] * (BLOCK // 128), axis=1)
            miss = jnp.where(same, -logit, logit)
            tail = jnp.exp2(-jnp.abs(logit))
            denominator = 1.0 + tail
            whole = pl.reciprocal(denominator, approx=True)
            whole = whole * (2.0 - denominator * whole)
            share = jnp.where(miss > 0, whole, tail * whole)
            coef[at : at + CHUNK, pl.ds(column, BLOCK)] = jnp.where(same, -share, share).astype(
                jnp.bfloat16
            )
            linear += jnp.maximum(miss, 0.0)
            product += tail * (1.0 + product)
        loss = jnp.sum(linear * (1.0 / LOG2E) + log1p(product), axis=0, keepdims=True)
        grad = dot(coef[:, pl.ds(column, BLOCK)], text[...], ((0,), (0,)))
        if first:
            image_out[...] = grad
            loss_out[...] = loss
        else:
            loss_out[...] = loss + loss_in[...]
            grad = scale * (grad + image_in[...])

            @pl.when(is_near)
            def _():
                own_out[...] = grad

            @pl.when(jnp.logical_not(is_near))
            def _():
                far_out[...] = grad.astype(jnp.bfloat16)

    @pl.when(step >= steps)
    def _():
        row = pl.multiple_of((step - steps) * BLOCK, BLOCK)
        rows = near.shape[0]
        total = dot(coef[pl.ds(row, BLOCK), :rows], near[...], ((1,), (0,)))
        total += dot(coef[pl.ds(row, BLOCK), rows:], far[...], ((1,), (0,)))
        text_out[...] = scale * total


def pair_call(params, image_ids, text_ids, near, far, text, partial=None):
    rows, width = near.shape
    text_rows = text.shape[0]
    steps = 2 * rows // BLOCK
    text_steps = text_rows // BLOCK
    half = steps // 2
    first = partial is None
    whole = lambda n: pl.BlockSpec((n, width), lambda s: (0, 0))
    by_step = lambda s: jnp.minimum(s, steps - 1)
    id_block = pl.BlockSpec((1, BLOCK), lambda s: (0, by_step(s)))
    block = lambda where: pl.BlockSpec((BLOCK, width), lambda s: (where(s), 0))
    in_specs = [
        pl.BlockSpec(memory_space=pltpu.SMEM),
        id_block,
        pl.BlockSpec((1, text_rows), lambda s: (0, 0)),
        whole(rows),
        whole(rows),
        whole(text_rows),
    ]
    args = [params, image_ids, text_ids, near, far, text]
    shape = jax.ShapeDtypeStruct
    loss_shape = shape((1, 2 * rows), jnp.float32)
    text_shape = shape((text_rows, width), jnp.float32)
    text_block = block(lambda s: jnp.maximum(s - steps, 0))
    if first:
        out_shape = [shape((2 * rows, width), jnp.float32), loss_shape, text_shape]
        out_specs = [block(by_step), id_block, text_block]
    else:
        in_specs += [block(by_step), id_block]
        args += partial
        out_shape = [
            shape((rows, width), jnp.float32), shape((rows, width), jnp.bfloat16), loss_shape, text_shape
        ]
        out_specs = [
            block(lambda s: jnp.minimum(s, half - 1)),
            block(lambda s: jnp.clip(s - half, 0, half - 1)),
            id_block,
            text_block,
        ]
    return pl.pallas_call(
        lambda *refs: pair_body(first, steps, text_rows, *refs),
        grid=(steps + text_steps,),
        in_specs=in_specs,
        out_specs=out_specs,
        out_shape=out_shape,
        scratch_shapes=[
            pltpu.VMEM((text_rows, 2 * rows), jnp.bfloat16),
            pltpu.VMEM((text_rows, 128), jnp.int32),
        ],
        compiler_params=pltpu.CompilerParams(
            vmem_limit_bytes=44 * 2**20, dimension_semantics=("arbitrary",)
        ),
        cost_estimate=pl.CostEstimate(
            flops=12 * rows * text_rows * width,
            bytes_accessed=20 * rows * width,
            transcendentals=4 * rows * text_rows,
        ),
    )(*args)


def xor_route(count, mask):
    return [(d, d ^ mask) for d in range(count)]


def partner_mask(rnd, width):
    return rnd * width ^ (rnd & 1) * (width // 2)


def solution(mesh):
    groups, width = mesh.shape["dp"], mesh.shape["narrow"]
    count, half = groups * width, width // 2
    over_z = xor_route(count, half)
    over_core = xor_route(count, 1)

    def forward(rnd, caption, picture, ids):
        text_own = lax.ppermute(caption, AXES, xor_route(count, partner_mask(rnd, width)))
        image_far = lax.ppermute(picture, AXES, over_z)
        rows = picture.shape[0]
        me = lax.axis_index("dp") * width + lax.axis_index("narrow")
        text_at = me ^ partner_mask(rnd, width)
        take = lambda device: lax.dynamic_slice_in_dim(ids, device * rows, rows)
        image_ids = jnp.concatenate([take(me), take(me ^ half)])
        return text_own, image_far, image_ids[None], take(text_at)[None], take(text_at ^ 1)[None]

    def backward(rnd, text_part, image_far_part, loss_far):
        loss_far = lax.ppermute(loss_far, AXES, over_z)
        text_grad = lax.ppermute(text_part, AXES, xor_route(count, partner_mask(rnd, width)))
        image_far_part = lax.ppermute(image_far_part, AXES, over_z)
        return text_grad, image_far_part, loss_far

    def by_round(step, which, *args):
        branches = [lambda *a, r=r: step(r, *a) for r in range(1, groups)]
        return lax.switch(which, branches, *args)

    def per_device(picture, caption, ids, rnd, scale, shift):
        which = rnd[0] - 1
        params = jnp.concatenate([scale, shift])
        rows = picture.shape[0]
        text_own, image_far, image_ids, own_ids, near_ids = by_round(
            forward, which, caption, picture, ids
        )
        text_near = lax.ppermute(text_own, AXES, over_core)
        *partial, near_part = pair_call(params, image_ids, near_ids, picture, image_far, text_near)
        near_part = lax.ppermute(near_part, AXES, over_core)
        image_grad, image_far_part, loss_sum, text_part = pair_call(
            params, image_ids, own_ids, picture, image_far, text_own, partial
        )
        text_part = (text_part + near_part).astype(jnp.bfloat16)
        text_grad, image_far_part, loss_far = by_round(
            backward, which, text_part, image_far_part, loss_sum[0, rows:]
        )
        image_grad = image_grad + image_far_part.astype(jnp.float32)
        row_loss = (loss_sum[0, :rows] + loss_far) / (rows * width)
        return image_grad, text_grad.astype(jnp.float32), row_loss

    in_specs = (P(AXES, None), P(AXES, None), P(), P(), P(), P())
    out_specs = (P(AXES, None), P(AXES, None), P(AXES))
    return jax.shard_map(
        per_device, mesh=mesh, in_specs=in_specs, out_specs=out_specs, check_vma=False
    )
```

```python
import jax
import jax.numpy as jnp
from jax import lax
from jax.experimental import pallas as pl
from jax.experimental.pallas import tpu as pltpu
from jax.sharding import PartitionSpec as P

AXES = ("dp", "narrow")
TEXTS, IMAGES = 384, 256
CHUNK = 16
COLUMNS = 256
ANY = pl.BlockSpec(memory_space=pl.ANY)


def dot(a, b, dims):
    return lax.dot_general(a, b, (dims, ((), ())), preferred_element_type=jnp.float32)


def log1p(q):
    small = q * (1.0 - q * (0.5 - q * (1.0 / 3.0 - q * 0.25)))
    return jnp.where(q < 0.01, small, jnp.log(1.0 + q))


def aligned(index, size):
    return pl.ds(pl.multiple_of(index * size, size), size)


def padded(width):
    return -(-width // COLUMNS) * COLUMNS


def pair_body(params, image_ids, text_ids, near, far, text, coef_out, text_out, loss_out,
              images, texts, raw, ids_column, coef, coef_turned, total, sems):
    rows, width = near.shape
    text_tiles = text.shape[0] // TEXTS
    tiles = 2 * rows // IMAGES * text_tiles
    copies = [
        pltpu.make_async_copy(near, images.at[:rows, :width], sems.at[0]),
        pltpu.make_async_copy(text, texts, sems.at[1]),
        pltpu.make_async_copy(far, images.at[rows:, :width], sems.at[2]),
    ]
    for copy in copies:
        copy.start()
    for k in range(text.shape[0] // 128):
        part = jnp.broadcast_to(text_ids[:, k * 128 : (k + 1) * 128], (128, 128))
        ids_column[k * 128 : (k + 1) * 128, :] = part.T
    scale, shift = params[0], params[1]

    def tile(k, _):
        @pl.when(k == 0)
        def _():
            copies[0].wait()
            copies[1].wait()

        @pl.when(k == tiles // 2)
        def _():
            copies[2].wait()

        done = jnp.maximum(k - 1, 0)
        image_at, text_at = lax.div(done, text_tiles), lax.rem(done, text_tiles)
        columns = aligned(image_at, IMAGES)
        left = jnp.broadcast_to(image_ids[:, columns], (CHUNK, IMAGES))
        linear = jnp.zeros((CHUNK, IMAGES), jnp.float32)
        product = jnp.zeros((CHUNK, IMAGES), jnp.float32)
        for group in range(0, TEXTS, 128):
            parts = []
            for at in range(group, group + 128, CHUNK):
                logit = raw[at : at + CHUNK, :] * scale + shift
                right = ids_column[pl.ds(pl.multiple_of(text_at * TEXTS + at, CHUNK), CHUNK), :]
                same = left == jnp.concatenate([right] * (IMAGES // 128), axis=1)
                minus = -logit
                miss = jnp.where(same, minus, logit)
                tail = jnp.exp(jnp.minimum(logit, minus))
                denominator = 1.0 + tail
                whole = pl.reciprocal(denominator, approx=True)
                whole = whole * (2.0 - denominator * whole)
                share = jnp.where(miss > 0, whole, tail * whole)
                parts.append(jnp.where(same, -share, share))
                linear += jnp.maximum(miss, 0.0)
                product += tail * (1.0 + product)
            block = jnp.concatenate(parts, axis=0)
            where = pl.ds(pl.multiple_of(text_at * TEXTS + group, 128), 128)
            coef[where, columns] = block.astype(jnp.bfloat16)
            coef_turned[columns, where] = block.T.astype(jnp.bfloat16)
        loss = jnp.sum(linear + log1p(product), axis=0, keepdims=True)
        loss_out[:, columns] = loss + jnp.where(text_at == 0, 0.0, loss_out[:, columns])

        now = jnp.minimum(k, tiles - 1)
        raw[...] = dot(
            texts[aligned(lax.rem(now, text_tiles), TEXTS), :],
            images[aligned(lax.div(now, text_tiles), IMAGES), :width],
            ((1,), (1,)),
        )
        return 0

    lax.fori_loop(0, tiles + 1, tile, 0)
    coef_copy = pltpu.make_async_copy(coef_turned, coef_out, sems.at[3])
    coef_copy.start()

    column_steps = images.shape[1] // COLUMNS

    def grad(k, _):
        row, column = lax.div(k, column_steps), lax.rem(k, column_steps)
        here = aligned(column, COLUMNS)
        total[aligned(row, TEXTS), here] = scale * dot(
            coef[aligned(row, TEXTS), :], images[:, here], ((1,), (0,))
        )
        return 0

    lax.fori_loop(0, text_tiles * column_steps, grad, 0)
    text_copy = pltpu.make_async_copy(total.at[:, :width], text_out, sems.at[0])
    text_copy.start()
    coef_copy.wait()
    text_copy.wait()


def pair_call(params, image_ids, text_ids, near, far, text):
    rows, width = near.shape
    text_rows = text.shape[0]
    shape = jax.ShapeDtypeStruct
    vmem = pl.BlockSpec(memory_space=pltpu.VMEM)
    return pl.pallas_call(
        pair_body,
        in_specs=[pl.BlockSpec(memory_space=pltpu.SMEM), vmem, vmem, ANY, ANY, ANY],
        out_specs=[ANY, ANY, vmem],
        out_shape=[
            shape((2 * rows, text_rows), jnp.bfloat16),
            shape((text_rows, width), jnp.float32),
            shape((1, 2 * rows), jnp.float32),
        ],
        scratch_shapes=[
            pltpu.VMEM((2 * rows, padded(width)), jnp.bfloat16),
            pltpu.VMEM((text_rows, width), jnp.bfloat16),
            pltpu.VMEM((TEXTS, IMAGES), jnp.float32),
            pltpu.VMEM((text_rows, 128), jnp.int32),
            pltpu.VMEM((text_rows, 2 * rows), jnp.bfloat16),
            pltpu.VMEM((2 * rows, text_rows), jnp.bfloat16),
            pltpu.VMEM((text_rows, padded(width)), jnp.float32),
            pltpu.SemaphoreType.DMA((4,)),
        ],
        compiler_params=pltpu.CompilerParams(vmem_limit_bytes=24 * 2**20),
        cost_estimate=pl.CostEstimate(
            flops=8 * rows * text_rows * width,
            bytes_accessed=20 * rows * width,
            transcendentals=4 * rows * text_rows,
        ),
    )(params, image_ids, text_ids, near, far, text)


def image_body(first_row, params, coef_a, coef_b, text_a, text_b, out, coef, texts, total, result, sems):
    rows, width = out.shape
    half = text_a.shape[0]
    mine = pl.ds(first_row, rows)
    copies = [
        pltpu.make_async_copy(coef_a.at[mine, :], coef.at[:, :half], sems.at[0]),
        pltpu.make_async_copy(coef_b.at[mine, :], coef.at[:, half:], sems.at[1]),
        pltpu.make_async_copy(text_a, texts.at[:half, :width], sems.at[2]),
        pltpu.make_async_copy(text_b, texts.at[half:, :width], sems.at[3]),
    ]
    for copy in copies:
        copy.start()
    for copy in copies:
        copy.wait()
    scale = params[0]
    column_steps = texts.shape[1] // COLUMNS

    def grad(k, _):
        row, column = lax.div(k, column_steps), lax.rem(k, column_steps)
        here = aligned(column, COLUMNS)
        sums = scale * dot(coef[aligned(row, TEXTS), :], texts[:, here], ((1,), (0,)))
        result[aligned(row, TEXTS), here] = sums.astype(result.dtype)
        return 0

    lax.fori_loop(0, rows // TEXTS * column_steps, grad, 0)
    copy = pltpu.make_async_copy(result.at[:, :width], out, sems.at[0])
    copy.start()
    copy.wait()


def image_call(params, coefs, texts, far, dtype):
    rows, width = texts[0].shape
    body = lambda p, ca, cb, ta, tb, out, coef, held, result, sems: image_body(
        rows if far else 0, p, ca, cb, ta, tb, out, coef, held, None, result, sems
    )
    return pl.pallas_call(
        body,
        in_specs=[pl.BlockSpec(memory_space=pltpu.SMEM), ANY, ANY, ANY, ANY],
        out_specs=ANY,
        out_shape=jax.ShapeDtypeStruct((rows, width), dtype),
        scratch_shapes=[
            pltpu.VMEM((rows, 2 * rows), jnp.bfloat16),
            pltpu.VMEM((2 * rows, padded(width)), jnp.bfloat16),
            pltpu.VMEM((rows, padded(width)), dtype),
            pltpu.SemaphoreType.DMA((4,)),
        ],
        compiler_params=pltpu.CompilerParams(vmem_limit_bytes=24 * 2**20),
        cost_estimate=pl.CostEstimate(
            flops=4 * rows * rows * width, bytes_accessed=12 * rows * width, transcendentals=0
        ),
    )(params, *coefs, *texts)


def xor_route(count, mask):
    return [(d, d ^ mask) for d in range(count)]


def partner_mask(rnd, width):
    return rnd * width ^ (rnd & 1) * (width // 2)


def solution(mesh):
    groups, width = mesh.shape["dp"], mesh.shape["narrow"]
    count, half = groups * width, width // 2
    over_z = xor_route(count, half)
    over_core = xor_route(count, 1)

    def forward(rnd, caption, picture, ids):
        text_own = lax.ppermute(caption, AXES, xor_route(count, partner_mask(rnd, width)))
        image_far = lax.ppermute(picture, AXES, over_z)
        rows = picture.shape[0]
        me = lax.axis_index("dp") * width + lax.axis_index("narrow")
        text_at = me ^ partner_mask(rnd, width)
        take = lambda device: lax.dynamic_slice_in_dim(ids, device * rows, rows)
        image_ids = jnp.concatenate([take(me), take(me ^ half)])
        return text_own, image_far, image_ids[None], take(text_at)[None], take(text_at ^ 1)[None]

    def backward(rnd, text_part, image_far_part, loss_far):
        loss_far = lax.ppermute(loss_far, AXES, over_z)
        text_grad = lax.ppermute(text_part, AXES, xor_route(count, partner_mask(rnd, width)))
        image_far_part = lax.ppermute(image_far_part, AXES, over_z)
        return text_grad, image_far_part, loss_far

    def by_round(step, which, *args):
        branches = [lambda *a, r=r: step(r, *a) for r in range(1, groups)]
        return lax.switch(which, branches, *args)

    def per_device(picture, caption, ids, rnd, scale, shift):
        which = rnd[0] - 1
        params = jnp.concatenate([scale, shift])
        rows = picture.shape[0]
        text_own, image_far, image_ids, own_ids, near_ids = by_round(
            forward, which, caption, picture, ids
        )
        text_near = lax.ppermute(text_own, AXES, over_core)
        near_coef, near_part, near_loss = pair_call(
            params, image_ids, near_ids, picture, image_far, text_near
        )
        near_part = lax.ppermute(near_part, AXES, over_core)
        own_coef, text_part, own_loss = pair_call(
            params, image_ids, own_ids, picture, image_far, text_own
        )
        coefs, texts = (near_coef, own_coef), (text_near, text_own)
        image_far_part = image_call(params, coefs, texts, True, jnp.bfloat16)
        image_grad = image_call(params, coefs, texts, False, jnp.float32)
        text_part = (text_part + near_part).astype(jnp.bfloat16)
        loss_sum = (near_loss + own_loss)[0]
        text_grad, image_far_part, loss_far = by_round(
            backward, which, text_part, image_far_part, loss_sum[rows:]
        )
        image_grad = image_grad + image_far_part.astype(jnp.float32)
        row_loss = (loss_sum[:rows] + loss_far) / (rows * width)
        return image_grad, text_grad.astype(jnp.float32), row_loss

    in_specs = (P(AXES, None), P(AXES, None), P(), P(), P(), P())
    out_specs = (P(AXES, None), P(AXES, None), P(AXES))
    return jax.shard_map(
        per_device, mesh=mesh, in_specs=in_specs, out_specs=out_specs, check_vma=False
    )
```

```python
import jax
import jax.numpy as jnp
from jax import lax
from jax.sharding import PartitionSpec as P

AXES = ("dp", "narrow")


def xor_route(count, mask):
    return [(d, d ^ mask) for d in range(count)]


def pair_terms(logits, left_ids, right_ids):
    same = left_ids[:, None] == right_ids[None, :]
    z = jnp.where(same, logits, -logits)
    tail = jnp.exp(-jnp.abs(z))
    pair_loss = jnp.maximum(-z, 0.0) + jnp.log1p(tail)
    share = jnp.where(z > 0, tail, 1.0) / (1.0 + tail)
    coef = jnp.where(same, -share, share).astype(jnp.bfloat16)
    return pair_loss, coef


def dot(a, b, dims):
    return lax.dot_general(a, b, (dims, ((), ())), preferred_element_type=jnp.float32)


def by_round(step, low, high, rnd, *args):
    if high - low == 1:
        return step(low, *args)
    middle = (low + high) // 2
    return lax.cond(
        rnd < middle,
        lambda *a: by_round(step, low, middle, rnd, *a),
        lambda *a: by_round(step, middle, high, rnd, *a),
        *args,
    )


def exchange_round(rnd, count, width, picture, caption, ids, scale, shift):
    rows = picture.shape[0]
    half = width // 2
    flip = half if rnd & 1 else 0
    route = xor_route(count, (rnd * width) | flip)
    over_z = xor_route(count, half)
    over_core = xor_route(count, 1)
    me = lax.axis_index("dp") * width + lax.axis_index("narrow")

    text_own = lax.ppermute(caption, AXES, route)
    image_far = lax.ppermute(picture, AXES, over_z)
    text_near = lax.ppermute(text_own, AXES, over_core)

    text_at = me ^ ((rnd * width) | flip)
    take = lambda device: lax.dynamic_slice_in_dim(ids, device * rows, rows)
    image_ids = jnp.concatenate([take(me), take(me ^ half)])
    text_ids = jnp.concatenate([take(text_at), take(text_at ^ 1)])
    images = jnp.concatenate([picture, image_far])
    texts = jnp.concatenate([text_own, text_near])

    logits = scale * dot(images, texts, ((1,), (1,))) + shift
    pair_loss, coef = pair_terms(logits, image_ids, text_ids)
    loss_sum = jnp.sum(pair_loss, axis=1)
    loss_far = lax.ppermute(loss_sum[rows:], AXES, over_z)

    text_far_part = scale * dot(coef[:, rows:], images, ((0,), (0,)))
    text_far_part = lax.ppermute(text_far_part, AXES, over_core)
    text_part = scale * dot(coef[:, :rows], images, ((0,), (0,)))
    text_part = (text_part + text_far_part).astype(jnp.bfloat16)
    text_grad = lax.ppermute(text_part, AXES, route).astype(jnp.float32)

    image_far_part = (scale * dot(coef[rows:], texts, ((1,), (0,)))).astype(jnp.bfloat16)
    image_far_part, loss_far = lax.optimization_barrier((image_far_part, loss_far))
    image_far_part = lax.ppermute(image_far_part, AXES, over_z)
    image_grad = scale * dot(coef[:rows], texts, ((1,), (0,))) + image_far_part.astype(jnp.float32)
    row_loss = (loss_sum[:rows] + loss_far) / (rows * width)
    return image_grad, text_grad, row_loss


def solution(mesh):
    groups, width = mesh.shape["dp"], mesh.shape["narrow"]
    count = groups * width

    def per_device(picture, caption, ids, rnd, scale, shift):
        step = lambda r, *args: exchange_round(r, count, width, *args)
        return by_round(step, 1, groups, rnd[0], picture, caption, ids, scale[0], shift[0])

    in_specs = (P(AXES, None), P(AXES, None), P(), P(), P(), P())
    out_specs = (P(AXES, None), P(AXES, None), P(AXES))
    return jax.shard_map(
        per_device, mesh=mesh, in_specs=in_specs, out_specs=out_specs, check_vma=False
    )
```

```python
import jax
import jax.numpy as jnp
from jax import lax
from jax.experimental import pallas as pl
from jax.experimental.pallas import tpu as pltpu
from jax.sharding import PartitionSpec as P

AXES = ("dp", "narrow")
TEXTS, IMAGES = 384, 256
CHUNK = 16
COLUMNS = 256
VMEM = pl.BlockSpec(memory_space=pltpu.VMEM)
SMEM = pl.BlockSpec(memory_space=pltpu.SMEM)


def dot(a, b, dims):
    return lax.dot_general(a, b, (dims, ((), ())), preferred_element_type=jnp.float32)


def log1p(q):
    small = q * (1.0 - q * (0.5 - q * (1.0 / 3.0 - q * 0.25)))
    return jnp.where(q < 0.01, small, jnp.log(1.0 + q))


def aligned(index, size):
    return pl.ds(pl.multiple_of(index * size, size), size)


def two_products(scale, left, right, out):
    rows, width = out.shape

    def step(k, _):
        here = aligned(k, TEXTS)
        a, b = left[0][here, :], left[1][here, :]
        for at in range(0, width, COLUMNS):
            to = slice(at, min(at + COLUMNS, width))
            sums = dot(a, right[0][:, to], ((1,), (0,))) + dot(b, right[1][:, to], ((1,), (0,)))
            out[here, to] = (scale * sums).astype(out.dtype)
        return 0

    lax.fori_loop(0, rows // TEXTS, step, 0)


def pair_body(params, image_ids, text_ids, near, far, text, coef_out, text_out, loss_out,
              raw, ids_column, coef):
    rows = near.shape[0]
    text_tiles = text.shape[0] // TEXTS
    blocks = rows // IMAGES
    tiles = 2 * blocks * text_tiles
    for k in range(text.shape[0] // 128):
        part = jnp.broadcast_to(text_ids[:, k * 128 : (k + 1) * 128], (128, 128))
        ids_column[k * 128 : (k + 1) * 128, :] = part.T
    scale, shift = params[0], params[1]

    def tile(k, _):
        now = jnp.minimum(k, tiles - 1)
        block = lax.div(now, text_tiles)
        here = aligned(lax.rem(block, blocks), IMAGES)
        images = jnp.where(block < blocks, near[here, :], far[here, :])
        coming = dot(text[aligned(lax.rem(now, text_tiles), TEXTS), :], images, ((1,), (1,)))

        done = jnp.maximum(k - 1, 0)
        image_at, text_at = lax.div(done, text_tiles), lax.rem(done, text_tiles)
        columns = aligned(image_at, IMAGES)
        left = jnp.broadcast_to(image_ids[:, columns], (CHUNK, IMAGES))
        linear = jnp.zeros((CHUNK, IMAGES), jnp.float32)
        product = jnp.zeros((CHUNK, IMAGES), jnp.float32)
        parts = []
        for at in range(0, TEXTS, CHUNK):
            logit = raw[at : at + CHUNK, :] * scale + shift
            right = ids_column[pl.ds(pl.multiple_of(text_at * TEXTS + at, CHUNK), CHUNK), :]
            same = left == jnp.concatenate([right] * (IMAGES // 128), axis=1)
            minus = -logit
            miss = jnp.where(same, minus, logit)
            tail = jnp.exp(jnp.minimum(logit, minus))
            denominator = 1.0 + tail
            whole = pl.reciprocal(denominator, approx=True)
            whole = whole * (2.0 - denominator * whole)
            share = jnp.where(miss > 0, whole, tail * whole)
            parts.append(jnp.where(same, -share, share).astype(jnp.bfloat16))
            linear += jnp.maximum(miss, 0.0)
            product += tail * (1.0 + product)
        loss = jnp.sum(linear + log1p(product), axis=0, keepdims=True)
        loss += jnp.where(text_at == 0, 0.0, loss_out[:, columns])

        found = jnp.concatenate(parts, axis=0)
        where = aligned(text_at, TEXTS)
        coef[where, columns] = found
        coef_out[columns, where] = found.T
        loss_out[:, columns] = loss
        raw[...] = coming
        return 0

    lax.fori_loop(0, tiles + 1, tile, 0)
    two_products(scale, (coef.at[:, :rows], coef.at[:, rows:]), (near, far), text_out)


def pair_call(params, image_ids, text_ids, near, far, text):
    rows, width = near.shape
    text_rows = text.shape[0]
    shape = jax.ShapeDtypeStruct
    return pl.pallas_call(
        pair_body,
        in_specs=[SMEM, VMEM, VMEM, VMEM, VMEM, VMEM],
        out_specs=[VMEM, VMEM, VMEM],
        out_shape=[
            shape((2 * rows, text_rows), jnp.bfloat16),
            shape((text_rows, width), jnp.float32),
            shape((1, 2 * rows), jnp.float32),
        ],
        scratch_shapes=[
            pltpu.VMEM((TEXTS, IMAGES), jnp.float32),
            pltpu.VMEM((text_rows, 128), jnp.int32),
            pltpu.VMEM((text_rows, 2 * rows), jnp.bfloat16),
        ],
        compiler_params=pltpu.CompilerParams(vmem_limit_bytes=24 * 2**20),
        cost_estimate=pl.CostEstimate(
            flops=8 * rows * text_rows * width,
            bytes_accessed=20 * rows * width,
            transcendentals=4 * rows * text_rows,
        ),
    )(params, image_ids, text_ids, near, far, text)


def image_call(params, coefs, texts, far, dtype):
    rows, width = texts[0].shape
    mine = pl.ds(rows if far else 0, rows)

    def body(params, coef_a, coef_b, text_a, text_b, out):
        two_products(params[0], (coef_a.at[mine, :], coef_b.at[mine, :]), (text_a, text_b), out)

    return pl.pallas_call(
        body,
        in_specs=[SMEM, VMEM, VMEM, VMEM, VMEM],
        out_specs=VMEM,
        out_shape=jax.ShapeDtypeStruct((rows, width), dtype),
        compiler_params=pltpu.CompilerParams(vmem_limit_bytes=24 * 2**20),
        cost_estimate=pl.CostEstimate(
            flops=4 * rows * rows * width, bytes_accessed=12 * rows * width, transcendentals=0
        ),
    )(params, *coefs, *texts)


def xor_route(count, mask):
    return [(d, d ^ mask) for d in range(count)]


def partner_mask(rnd, width):
    return rnd * width ^ (rnd & 1) * (width // 2)


def solution(mesh):
    groups, width = mesh.shape["dp"], mesh.shape["narrow"]
    count, half = groups * width, width // 2
    over_z = xor_route(count, half)
    over_core = xor_route(count, 1)

    def forward(rnd, caption, picture, ids):
        text_own = lax.ppermute(caption, AXES, xor_route(count, partner_mask(rnd, width)))
        image_far = lax.ppermute(picture, AXES, over_z)
        rows = picture.shape[0]
        me = lax.axis_index("dp") * width + lax.axis_index("narrow")
        text_at = me ^ partner_mask(rnd, width)
        take = lambda device: lax.dynamic_slice_in_dim(ids, device * rows, rows)
        image_ids = jnp.concatenate([take(me), take(me ^ half)])
        return text_own, image_far, image_ids[None], take(text_at)[None], take(text_at ^ 1)[None]

    def backward(rnd, text_part, image_far_part, loss_far):
        loss_far = lax.ppermute(loss_far, AXES, over_z)
        text_grad = lax.ppermute(text_part, AXES, xor_route(count, partner_mask(rnd, width)))
        image_far_part = lax.ppermute(image_far_part, AXES, over_z)
        return text_grad, image_far_part, loss_far

    def by_round(step, which, *args):
        branches = [lambda *a, r=r: step(r, *a) for r in range(1, groups)]
        return lax.switch(which, branches, *args)

    def per_device(picture, caption, ids, rnd, scale, shift):
        which = rnd[0] - 1
        params = jnp.concatenate([scale, shift])
        rows = picture.shape[0]
        text_own, image_far, image_ids, own_ids, near_ids = by_round(
            forward, which, caption, picture, ids
        )
        text_near = lax.ppermute(text_own, AXES, over_core)
        near_coef, near_part, near_loss = pair_call(
            params, image_ids, near_ids, picture, image_far, text_near
        )
        near_part = lax.ppermute(near_part, AXES, over_core)
        own_coef, text_part, own_loss = pair_call(
            params, image_ids, own_ids, picture, image_far, text_own
        )
        coefs, texts = (near_coef, own_coef), (text_near, text_own)
        image_far_part = image_call(params, coefs, texts, True, jnp.bfloat16)
        image_grad = image_call(params, coefs, texts, False, jnp.float32)
        text_part = (text_part + near_part).astype(jnp.bfloat16)
        loss_sum = (near_loss + own_loss)[0]
        text_grad, image_far_part, loss_far = by_round(
            backward, which, text_part, image_far_part, loss_sum[rows:]
        )
        image_grad = image_grad + image_far_part.astype(jnp.float32)
        row_loss = (loss_sum[:rows] + loss_far) / (rows * width)
        return image_grad, text_grad.astype(jnp.float32), row_loss

    in_specs = (P(AXES, None), P(AXES, None), P(), P(), P(), P())
    out_specs = (P(AXES, None), P(AXES, None), P(AXES))
    return jax.shard_map(
        per_device, mesh=mesh, in_specs=in_specs, out_specs=out_specs, check_vma=False
    )
```

```python
import jax
import jax.numpy as jnp
from jax import lax
from jax.experimental import pallas as pl
from jax.experimental.pallas import tpu as pltpu
from jax.sharding import PartitionSpec as P

AXES = ("dp", "narrow")
TEXTS, IMAGES = 384, 256
CHUNK = 16
ROWS = 256
FAN = 6
VMEM = pl.BlockSpec(memory_space=pltpu.VMEM)
SMEM = pl.BlockSpec(memory_space=pltpu.SMEM)
LIMIT = pltpu.CompilerParams(vmem_limit_bytes=20 * 2**20)


def dot(a, b, dims=((1,), (0,))):
    return lax.dot_general(a, b, (dims, ((), ())), preferred_element_type=jnp.float32)


def log1p(q):
    small = q * (1.0 - q * (0.5 - q * (1.0 / 3.0 - q * 0.25)))
    return jnp.where(q < 0.01, small, jnp.log(1.0 + q))


def aligned(index, size):
    return pl.ds(pl.multiple_of(index * size, size), size)


def pair_tiles(params, image_ids, text_ids, turned, text, coef_out, coef_turned_out, loss_out, raw, ids_column):
    text_tiles = text.shape[0] // TEXTS
    tiles = turned.shape[1] // IMAGES * text_tiles
    for k in range(text.shape[0] // 128):
        part = jnp.broadcast_to(text_ids[:, k * 128 : (k + 1) * 128], (128, 128))
        ids_column[k * 128 : (k + 1) * 128, :] = part.T
    scale, shift = params[0], params[1]

    def tile(k, _):
        now = jnp.minimum(k, tiles - 1)
        coming = dot(
            text[aligned(lax.rem(now, text_tiles), TEXTS), :],
            turned[:, aligned(lax.div(now, text_tiles), IMAGES)],
        )

        done = jnp.maximum(k - 1, 0)
        image_at, text_at = lax.div(done, text_tiles), lax.rem(done, text_tiles)
        columns = aligned(image_at, IMAGES)
        left = jnp.broadcast_to(image_ids[:, columns], (CHUNK, IMAGES))
        linear = jnp.zeros((CHUNK, IMAGES), jnp.float32)
        product = jnp.zeros((CHUNK, IMAGES), jnp.float32)
        parts = []
        for at in range(0, TEXTS, CHUNK):
            logit = raw[at : at + CHUNK, :] * scale + shift
            right = ids_column[pl.ds(pl.multiple_of(text_at * TEXTS + at, CHUNK), CHUNK), :]
            same = left == jnp.concatenate([right] * (IMAGES // 128), axis=1)
            minus = -logit
            miss = jnp.where(same, minus, logit)
            tail = jnp.exp(jnp.minimum(logit, minus))
            denominator = 1.0 + tail
            whole = pl.reciprocal(denominator, approx=True)
            whole = whole * (2.0 - denominator * whole)
            share = jnp.where(miss > 0, whole, tail * whole)
            parts.append(jnp.where(same, -share, share).astype(jnp.bfloat16))
            linear += jnp.maximum(miss, 0.0)
            product += tail * (1.0 + product)
        loss = jnp.sum(linear + log1p(product), axis=0, keepdims=True)
        loss += jnp.where(text_at == 0, 0.0, loss_out[:, columns])

        found = jnp.concatenate(parts, axis=0)
        where = aligned(text_at, TEXTS)
        coef_out[where, columns] = found
        coef_turned_out[columns, where] = found.T
        loss_out[:, columns] = loss
        raw[...] = coming
        return 0

    lax.fori_loop(0, tiles + 1, tile, 0)


def pair_call(params, image_ids, text_ids, images, text):
    text_rows, width = text.shape
    shape = jax.ShapeDtypeStruct
    turn = len(images) == 2
    count = sum(block.shape[0] for block in images) if turn else images[0].shape[1]

    def body(params, image_ids, text_ids, *refs):
        if turn:
            near, far, text, coef, coef_turned, loss, turned, raw, ids_column = refs
            blocks = near.shape[0] // IMAGES

            def step(k, _):
                turned[:, aligned(k, IMAGES)] = near[aligned(k, IMAGES), :].T
                turned[:, aligned(k + blocks, IMAGES)] = far[aligned(k, IMAGES), :].T
                return 0

            lax.fori_loop(0, blocks, step, 0)
        else:
            turned, text, coef, coef_turned, loss, raw, ids_column = refs
        pair_tiles(params, image_ids, text_ids, turned, text, coef, coef_turned, loss, raw, ids_column)

    out_shape = [
        shape((text_rows, count), jnp.bfloat16),
        shape((count, text_rows), jnp.bfloat16),
        shape((1, count), jnp.float32),
    ]
    if turn:
        out_shape.append(shape((width, count), jnp.bfloat16))
    return pl.pallas_call(
        body,
        in_specs=[SMEM] + [VMEM] * (3 + len(images)),
        out_specs=[VMEM] * len(out_shape),
        out_shape=out_shape,
        scratch_shapes=[
            pltpu.VMEM((TEXTS, IMAGES), jnp.float32),
            pltpu.VMEM((text_rows, 128), jnp.int32),
        ],
        compiler_params=LIMIT,
        cost_estimate=pl.CostEstimate(
            flops=2 * count * text_rows * width,
            bytes_accessed=4 * count * width,
            transcendentals=2 * count * text_rows,
        ),
    )(params, image_ids, text_ids, *images, text)


def grad_call(params, lefts, at, rights, dtype):
    rows, width = rights[0].shape

    def body(params, left_a, left_b, right_a, right_b, out):
        scale = params[0]

        def step(k, _):
            here = aligned(k, ROWS)
            sums = 0.0
            for left, right, (row, column) in zip((left_a, left_b), (right_a, right_b), at):
                rows_here = pl.ds(pl.multiple_of(row + k * ROWS, ROWS), ROWS)
                sums += dot(left[rows_here, column : column + right.shape[0]], right[...])
            out[here, :] = (scale * sums).astype(out.dtype)
            return 0

        lax.fori_loop(0, rows // ROWS, step, 0)

    return pl.pallas_call(
        body,
        in_specs=[SMEM] + [VMEM] * 4,
        out_specs=VMEM,
        out_shape=jax.ShapeDtypeStruct((rows, width), dtype),
        compiler_params=LIMIT,
        cost_estimate=pl.CostEstimate(
            flops=4 * rows * rows * width, bytes_accessed=12 * rows * width, transcendentals=0
        ),
    )(params, *lefts, *rights)


def final_call(image_grad, image_far_part, text_grad):
    rows, width = image_grad.shape

    def body(image_grad, image_far_part, text_grad, image_out, text_out):
        image_out[...] = image_grad[...] + image_far_part[...].astype(jnp.float32)
        text_out[...] = text_grad[...].astype(jnp.float32)

    block = pl.BlockSpec((128, width), lambda s: (s, 0))
    return pl.pallas_call(
        body,
        grid=(rows // 128,),
        in_specs=[block] * 3,
        out_specs=[block] * 2,
        out_shape=[jax.ShapeDtypeStruct((rows, width), jnp.float32)] * 2,
        compiler_params=LIMIT,
        cost_estimate=pl.CostEstimate(
            flops=rows * width, bytes_accessed=16 * rows * width, transcendentals=0
        ),
    )(image_grad, image_far_part, text_grad)


def xor_route(count, mask):
    return [(d, d ^ mask) for d in range(count)]


def partner_mask(rnd, width):
    return rnd * width ^ (rnd & 1) * (width // 2)


def by_round(step, low, high, rnd, *args):
    if high - low == 1:
        return step(low, *args)
    size = -(-(high - low) // FAN)
    starts = list(range(low, high, size))
    branches = [
        lambda *a, s=s: by_round(step, s, min(s + size, high), rnd, *a) for s in starts
    ]
    return lax.switch(lax.div(rnd - low, jnp.int32(size)), branches, *args)


def solution(mesh):
    groups, width = mesh.shape["dp"], mesh.shape["narrow"]
    count, half = groups * width, width // 2
    over_z = xor_route(count, half)
    over_core = xor_route(count, 1)

    def forward(rnd, caption, picture):
        text_own = lax.ppermute(caption, AXES, xor_route(count, partner_mask(rnd, width)))
        image_far = lax.ppermute(picture, AXES, over_z)
        return text_own, image_far

    def backward(rnd, text_part, image_far_part, loss_far):
        loss_far = lax.ppermute(loss_far, AXES, over_z)
        text_grad = lax.ppermute(text_part, AXES, xor_route(count, partner_mask(rnd, width)))
        image_far_part = lax.ppermute(image_far_part, AXES, over_z)
        return text_grad, image_far_part, loss_far

    def per_device(picture, caption, ids, rnd, scale, shift):
        rnd = rnd[0]
        params = jnp.concatenate([scale, shift])
        rows = picture.shape[0]
        me = lax.axis_index("dp") * width + lax.axis_index("narrow")
        text_at = me ^ partner_mask(rnd, width)
        take = lambda device: lax.dynamic_slice_in_dim(ids, device * rows, rows)
        image_ids = jnp.concatenate([take(me), take(me ^ half)])[None]
        own_ids, near_ids = take(text_at)[None], take(text_at ^ 1)[None]

        text_own, image_far = by_round(forward, 1, groups, rnd, caption, picture)
        images = (picture, image_far)
        text_near = lax.ppermute(text_own, AXES, over_core)
        own_coef, own_turned, own_loss, turned = pair_call(params, image_ids, own_ids, images, text_own)
        near_coef, near_turned, near_loss = pair_call(params, image_ids, near_ids, (turned,), text_near)
        loss_sum = own_loss + near_loss
        to_images = ((0, 0), (0, rows))
        near_part = grad_call(params, (near_coef,) * 2, to_images, images, jnp.float32)
        near_part = lax.ppermute(near_part, AXES, over_core)
        text_part = grad_call(params, (own_coef,) * 2, to_images, images, jnp.float32)
        turns, texts = (near_turned, own_turned), (text_near, text_own)
        image_far_part = grad_call(params, turns, ((rows, 0),) * 2, texts, jnp.bfloat16)
        image_grad = grad_call(params, turns, ((0, 0),) * 2, texts, jnp.float32)
        text_part = (text_part + near_part).astype(jnp.bfloat16)

        text_grad, image_far_part, loss_far = by_round(
            backward, 1, groups, rnd, text_part, image_far_part, loss_sum[0, rows:]
        )
        row_loss = (loss_sum[0, :rows] + loss_far) / (rows * width)
        return *final_call(image_grad, image_far_part, text_grad), row_loss

    in_specs = (P(AXES, None), P(AXES, None), P(), P(), P(), P())
    out_specs = (P(AXES, None), P(AXES, None), P(AXES))
    return jax.shard_map(
        per_device, mesh=mesh, in_specs=in_specs, out_specs=out_specs, check_vma=False
    )
```

```python
import jax
import jax.numpy as jnp
from jax import lax
from jax.sharding import PartitionSpec as P

AXES = ("dp", "narrow")


def xor_route(count, mask):
    return [(d, d ^ mask) for d in range(count)]


def pair_terms(logits, left_ids, right_ids):
    same = left_ids[:, None] == right_ids[None, :]
    z = jnp.where(same, logits, -logits)
    tail = jnp.exp(-jnp.abs(z))
    pair_loss = jnp.maximum(-z, 0.0) + jnp.log1p(tail)
    share = jnp.where(z > 0, tail, 1.0) / (1.0 + tail)
    coef = jnp.where(same, -share, share).astype(jnp.bfloat16)
    return pair_loss, coef


def dot(a, b, dims):
    return lax.dot_general(a, b, (dims, ((), ())), preferred_element_type=jnp.float32)


def partner_mask(rnd, width):
    return rnd * width ^ (rnd & 1) * (width // 2)


def solution(mesh):
    groups, width = mesh.shape["dp"], mesh.shape["narrow"]
    count, half = groups * width, width // 2
    over_z = xor_route(count, half)
    over_core = xor_route(count, 1)

    def forward(rnd, caption, picture):
        text_own = lax.ppermute(caption, AXES, xor_route(count, partner_mask(rnd, width)))
        image_far = lax.ppermute(picture, AXES, over_z)
        return text_own, image_far

    def backward(rnd, text_part, image_far_part, loss_far):
        loss_far = lax.ppermute(loss_far, AXES, over_z)
        text_grad = lax.ppermute(text_part, AXES, xor_route(count, partner_mask(rnd, width)))
        image_far_part = lax.ppermute(image_far_part, AXES, over_z)
        return text_grad, image_far_part, loss_far

    def by_round(step, which, *args):
        branches = [lambda *a, r=r: step(r, *a) for r in range(1, groups)]
        return lax.switch(which, branches, *args)

    def per_device(picture, caption, ids, rnd, scale, shift):
        rnd, scale, shift = rnd[0], scale[0], shift[0]
        rows = picture.shape[0]
        me = lax.axis_index("dp") * width + lax.axis_index("narrow")
        text_at = me ^ partner_mask(rnd, width)
        take = lambda device: lax.dynamic_slice_in_dim(ids, device * rows, rows)
        image_ids = jnp.concatenate([take(me), take(me ^ half)])
        text_ids = jnp.concatenate([take(text_at), take(text_at ^ 1)])

        text_own, image_far = by_round(forward, rnd - 1, caption, picture)
        text_near = lax.ppermute(text_own, AXES, over_core)
        images = jnp.concatenate([picture, image_far])
        texts = jnp.concatenate([text_own, text_near])

        logits = scale * dot(images, texts, ((1,), (1,))) + shift
        pair_loss, coef = pair_terms(logits, image_ids, text_ids)
        loss_sum = jnp.sum(pair_loss, axis=1)

        text_parts = lax.optimization_barrier(scale * dot(coef, images, ((0,), (0,))))
        text_far_part = lax.ppermute(text_parts[rows:], AXES, over_core)
        image_parts = lax.optimization_barrier(scale * dot(coef, texts, ((1,), (0,))))
        image_grad, image_far_part = image_parts[:rows], image_parts[rows:].astype(jnp.bfloat16)
        text_part = (text_parts[:rows] + text_far_part).astype(jnp.bfloat16)

        sent = lax.optimization_barrier((text_part, image_far_part, loss_sum[rows:]))
        text_grad, image_far_part, loss_far = by_round(backward, rnd - 1, *sent)
        image_grad = image_grad + image_far_part.astype(jnp.float32)
        row_loss = (loss_sum[:rows] + loss_far) / (rows * width)
        return image_grad, text_grad.astype(jnp.float32), row_loss

    in_specs = (P(AXES, None), P(AXES, None), P(), P(), P(), P())
    out_specs = (P(AXES, None), P(AXES, None), P(AXES))
    return jax.shard_map(
        per_device, mesh=mesh, in_specs=in_specs, out_specs=out_specs, check_vma=False
    )
```

```python
import jax
import jax.numpy as jnp
from jax import lax
from jax.sharding import PartitionSpec as P

AXES = ("dp", "narrow")


def xor_route(count, mask):
    return [(d, d ^ mask) for d in range(count)]


def pair_terms(logits, left_ids, right_ids):
    same = left_ids[:, None] == right_ids[None, :]
    z = jnp.where(same, logits, -logits)
    tail = jnp.exp(-jnp.abs(z))
    pair_loss = jnp.maximum(-z, 0.0) + jnp.log1p(tail)
    share = jnp.where(z > 0, tail, 1.0) / (1.0 + tail)
    coef = jnp.where(same, -share, share).astype(jnp.bfloat16)
    return pair_loss, coef


def dot(a, b, dims):
    return lax.dot_general(a, b, (dims, ((), ())), preferred_element_type=jnp.float32)


def partner_mask(rnd, width):
    return rnd * width ^ (rnd & 1) * (width // 2)


def solution(mesh):
    groups, width = mesh.shape["dp"], mesh.shape["narrow"]
    count, half = groups * width, width // 2
    over_z = xor_route(count, half)
    over_core = xor_route(count, 1)

    def over_dp(rnd, block):
        return lax.ppermute(block, AXES, xor_route(count, partner_mask(rnd, width)))

    def by_round(step, which, *args):
        branches = [lambda *a, r=r: step(r, *a) for r in range(1, groups)]
        return lax.switch(which, branches, *args)

    def per_device(picture, caption, ids, rnd, scale, shift):
        rnd, scale, shift = rnd[0], scale[0], shift[0]
        rows = picture.shape[0]
        me = lax.axis_index("dp") * width + lax.axis_index("narrow")
        text_at = me ^ partner_mask(rnd, width)
        take = lambda device: lax.dynamic_slice_in_dim(ids, device * rows, rows)
        image_ids = jnp.concatenate([take(me), take(me ^ half)])
        text_ids = jnp.concatenate([take(text_at), take(text_at ^ 1)])

        image_far = lax.ppermute(picture, AXES, over_z)
        text_own = by_round(over_dp, rnd - 1, caption)
        text_near = lax.ppermute(text_own, AXES, over_core)
        images = jnp.concatenate([picture, image_far])
        texts = jnp.concatenate([text_own, text_near])

        logits = scale * dot(images, texts, ((1,), (1,))) + shift
        pair_loss, coef = pair_terms(logits, image_ids, text_ids)
        loss_sum = jnp.sum(pair_loss, axis=1)

        text_parts = lax.optimization_barrier(scale * dot(coef, images, ((0,), (0,))))
        text_far_part = lax.ppermute(text_parts[rows:], AXES, over_core)
        image_parts = lax.optimization_barrier(scale * dot(coef, texts, ((1,), (0,))))
        image_grad, image_far_part = image_parts[:rows], image_parts[rows:].astype(jnp.bfloat16)
        text_part = (text_parts[:rows] + text_far_part).astype(jnp.bfloat16)

        loss_far = lax.ppermute(loss_sum[rows:], AXES, over_z)
        image_far_part, loss_far = lax.optimization_barrier((image_far_part, loss_far))
        image_far_part = lax.ppermute(image_far_part, AXES, over_z)
        text_grad = by_round(over_dp, rnd - 1, text_part)
        text_grad, image_far_part = lax.optimization_barrier((text_grad, image_far_part))
        image_grad = image_grad + image_far_part.astype(jnp.float32)
        row_loss = (loss_sum[:rows] + loss_far) / (rows * width)
        return image_grad, text_grad.astype(jnp.float32), row_loss

    in_specs = (P(AXES, None), P(AXES, None), P(), P(), P(), P())
    out_specs = (P(AXES, None), P(AXES, None), P(AXES))
    return jax.shard_map(
        per_device, mesh=mesh, in_specs=in_specs, out_specs=out_specs, check_vma=False
    )
```

```python
import jax
import jax.numpy as jnp
from jax import lax
from jax.experimental import pallas as pl
from jax.experimental.pallas import tpu as pltpu
from jax.sharding import PartitionSpec as P

AXES = ("dp", "narrow")
FINAL_ROWS = 192


def xor_route(count, mask):
    return [(d, d ^ mask) for d in range(count)]


def log1p(q):
    small = q * (1.0 - q * (0.5 - q * (1.0 / 3.0)))
    return jnp.where(q < 0.01, small, jnp.log(1.0 + q))


def pair_terms(logits, left_ids, right_ids):
    same = left_ids[:, None] == right_ids[None, :]
    z = jnp.where(same, logits, -logits)
    pair_loss = jnp.maximum(-z, 0.0) + log1p(jnp.exp(-jnp.abs(logits)))
    share = jnp.exp(-(pair_loss + z))
    coef = jnp.where(same, -share, share).astype(jnp.bfloat16)
    return pair_loss, coef


def dot(a, b, dims):
    return lax.dot_general(a, b, (dims, ((), ())), preferred_element_type=jnp.float32)


def final_call(image_parts, image_far_part, text_grad):
    rows, width = text_grad.shape

    def body(image_part, image_far_part, text_grad, image_out, text_out):
        image_out[...] = image_part[...] + image_far_part[...].astype(jnp.float32)
        text_out[...] = text_grad[...].astype(jnp.float32)

    block = pl.BlockSpec((FINAL_ROWS, width), lambda s: (s, 0))
    return pl.pallas_call(
        body,
        grid=(rows // FINAL_ROWS,),
        in_specs=[block] * 3,
        out_specs=[block] * 2,
        out_shape=[jax.ShapeDtypeStruct((rows, width), jnp.float32)] * 2,
        compiler_params=pltpu.CompilerParams(vmem_limit_bytes=20 * 2**20),
        cost_estimate=pl.CostEstimate(
            flops=rows * width, bytes_accessed=16 * rows * width, transcendentals=0
        ),
    )(image_parts, image_far_part, text_grad)


def partner_mask(rnd, width):
    return rnd * width ^ (rnd & 1) * (width // 2)


def solution(mesh):
    groups, width = mesh.shape["dp"], mesh.shape["narrow"]
    count, half = groups * width, width // 2
    over_z = xor_route(count, half)
    over_core = xor_route(count, 1)

    def over_dp(rnd, block):
        return lax.ppermute(block, AXES, xor_route(count, partner_mask(rnd, width)))

    def by_round(step, which, *args):
        branches = [lambda *a, r=r: step(r, *a) for r in range(1, groups)]
        return lax.switch(which, branches, *args)

    def per_device(picture, caption, ids, rnd, scale, shift):
        rnd, scale, shift = rnd[0], scale[0], shift[0]
        rows = picture.shape[0]
        me = lax.axis_index("dp") * width + lax.axis_index("narrow")
        text_at = me ^ partner_mask(rnd, width)
        take = lambda device: lax.dynamic_slice_in_dim(ids, device * rows, rows)
        image_ids = jnp.concatenate([take(me), take(me ^ half)])
        text_ids = jnp.concatenate([take(text_at), take(text_at ^ 1)])

        image_far = lax.ppermute(picture, AXES, over_z)
        text_own = by_round(over_dp, rnd - 1, caption)
        text_near = lax.ppermute(text_own, AXES, over_core)
        images = jnp.concatenate([picture, image_far])
        texts = jnp.concatenate([text_own, text_near])

        logits = scale * dot(images, texts, ((1,), (1,))) + shift
        pair_loss, coef = pair_terms(logits, image_ids, text_ids)
        loss_sum = jnp.sum(pair_loss, axis=1)

        text_parts = lax.optimization_barrier(scale * dot(coef, images, ((0,), (0,))))
        text_far_part = lax.ppermute(text_parts[rows:], AXES, over_core)
        image_parts = lax.optimization_barrier(scale * dot(coef, texts, ((1,), (0,))))
        image_far_part = image_parts[rows:].astype(jnp.bfloat16)
        text_part = (text_parts[:rows] + text_far_part).astype(jnp.bfloat16)

        loss_far = lax.ppermute(loss_sum[rows:], AXES, over_z)
        image_far_part, loss_far = lax.optimization_barrier((image_far_part, loss_far))
        image_far_part = lax.ppermute(image_far_part, AXES, over_z)
        text_grad = by_round(over_dp, rnd - 1, text_part)
        text_grad, image_far_part = lax.optimization_barrier((text_grad, image_far_part))
        image_grad, text_grad = final_call(image_parts, image_far_part, text_grad)
        row_loss = (loss_sum[:rows] + loss_far) / (rows * width)
        return image_grad, text_grad, row_loss

    in_specs = (P(AXES, None), P(AXES, None), P(), P(), P(), P())
    out_specs = (P(AXES, None), P(AXES, None), P(AXES))
    return jax.shard_map(
        per_device, mesh=mesh, in_specs=in_specs, out_specs=out_specs, check_vma=False
    )
```

```python
import jax
import jax.numpy as jnp
from jax import lax
from jax.experimental import pallas as pl
from jax.experimental.pallas import tpu as pltpu
from jax.sharding import PartitionSpec as P

AXES = ("dp", "narrow")
LOG1P = (
    0.99999994, -0.499994934, 0.333190948, -0.248429745, 0.191059798,
    -0.136631876, 0.0782252625, -0.0295048114, 0.00523258746,
)
FINAL_ROWS = 192


def xor_route(count, mask):
    return [(d, d ^ mask) for d in range(count)]


def log1p(q):
    ratio = jnp.full_like(q, LOG1P[-1])
    for factor in LOG1P[-2::-1]:
        ratio = ratio * q + factor
    return q * ratio


def pair_terms(logits, left_ids, right_ids):
    same = left_ids[:, None] == right_ids[None, :]
    z = jnp.where(same, logits, -logits)
    pair_loss = jnp.maximum(-z, 0.0) + log1p(jnp.exp(-jnp.abs(logits)))
    share = jnp.exp(-(pair_loss + z))
    coef = jnp.where(same, -share, share).astype(jnp.bfloat16)
    return pair_loss, coef


def dot(a, b, dims):
    return lax.dot_general(a, b, (dims, ((), ())), preferred_element_type=jnp.float32)


def final_call(image_parts, image_far_part, text_grad):
    rows, width = text_grad.shape

    def body(image_part, image_far_part, text_grad, image_out, text_out):
        image_out[...] = image_part[...] + image_far_part[...].astype(jnp.float32)
        text_out[...] = text_grad[...].astype(jnp.float32)

    block = pl.BlockSpec((FINAL_ROWS, width), lambda s: (s, 0))
    return pl.pallas_call(
        body,
        grid=(rows // FINAL_ROWS,),
        in_specs=[block] * 3,
        out_specs=[block] * 2,
        out_shape=[jax.ShapeDtypeStruct((rows, width), jnp.float32)] * 2,
        compiler_params=pltpu.CompilerParams(vmem_limit_bytes=58 * 2**20),
        cost_estimate=pl.CostEstimate(
            flops=rows * width, bytes_accessed=16 * rows * width, transcendentals=0
        ),
    )(image_parts, image_far_part, text_grad)


def partner_mask(rnd, width):
    return rnd * width ^ (rnd & 1) * (width // 2)


def solution(mesh):
    groups, width = mesh.shape["dp"], mesh.shape["narrow"]
    count, half = groups * width, width // 2
    over_z = xor_route(count, half)
    over_core = xor_route(count, 1)

    def over_dp(rnd, block):
        return lax.ppermute(block, AXES, xor_route(count, partner_mask(rnd, width)))

    def by_round(step, which, *args):
        branches = [lambda *a, r=r: step(r, *a) for r in range(1, groups)]
        return lax.switch(which, branches, *args)

    def per_device(picture, caption, ids, rnd, scale, shift):
        rnd, scale, shift = rnd[0], scale[0], shift[0]
        rows = picture.shape[0]
        me = lax.axis_index("dp") * width + lax.axis_index("narrow")
        text_at = me ^ partner_mask(rnd, width)
        take = lambda device: lax.dynamic_slice_in_dim(ids, device * rows, rows)
        image_ids = jnp.concatenate([take(me), take(me ^ half)])
        text_ids = jnp.concatenate([take(text_at), take(text_at ^ 1)])

        image_far = lax.ppermute(picture, AXES, over_z)
        text_own = by_round(over_dp, rnd - 1, caption)
        text_near = lax.ppermute(text_own, AXES, over_core)
        images = jnp.concatenate([picture, image_far])
        texts = jnp.concatenate([text_own, text_near])

        logits = scale * dot(images, texts, ((1,), (1,))) + shift
        pair_loss, coef = pair_terms(logits, image_ids, text_ids)
        loss_sum = jnp.sum(pair_loss, axis=1)

        text_parts = lax.optimization_barrier(scale * dot(coef, images, ((0,), (0,))))
        text_far_part = lax.ppermute(text_parts[rows:], AXES, over_core)
        image_parts = lax.optimization_barrier(scale * dot(coef, texts, ((1,), (0,))))
        image_far_part = image_parts[rows:].astype(jnp.bfloat16)
        text_part = (text_parts[:rows] + text_far_part).astype(jnp.bfloat16)

        loss_far = lax.ppermute(loss_sum[rows:], AXES, over_z)
        image_far_part, loss_far = lax.optimization_barrier((image_far_part, loss_far))
        image_far_part = lax.ppermute(image_far_part, AXES, over_z)
        text_grad = by_round(over_dp, rnd - 1, text_part)
        text_grad, image_far_part = lax.optimization_barrier((text_grad, image_far_part))
        image_grad, text_grad = final_call(image_parts, image_far_part, text_grad)
        row_loss = (loss_sum[:rows] + loss_far) / (rows * width)
        return image_grad, text_grad, row_loss

    in_specs = (P(AXES, None), P(AXES, None), P(), P(), P(), P())
    out_specs = (P(AXES, None), P(AXES, None), P(AXES))
    return jax.shard_map(
        per_device, mesh=mesh, in_specs=in_specs, out_specs=out_specs, check_vma=False
    )
```

```python
import jax
import jax.numpy as jnp
from jax import lax
from jax.experimental import pallas as pl
from jax.experimental.pallas import tpu as pltpu
from jax.sharding import PartitionSpec as P

AXES = ("dp", "narrow")
CHUNKS = 4


def xor_route(count, mask):
    return [(d, d ^ mask) for d in range(count)]


def pair_terms(logits, left_ids, right_ids):
    same = left_ids[:, None] == right_ids[None, :]
    z = jnp.where(same, logits, -logits)
    tail = jnp.exp(-jnp.abs(z))
    pair_loss = jnp.maximum(-z, 0.0) + jnp.log1p(tail)
    share = jnp.where(z > 0, tail, 1.0) / (1.0 + tail)
    coef = jnp.where(same, -share, share).astype(jnp.bfloat16)
    return pair_loss, coef


def dot(a, b, dims):
    return lax.dot_general(a, b, (dims, ((), ())), preferred_element_type=jnp.float32)


def final_call(image_parts, image_far_part, text_grad, loss_sum, loss_far, count):
    rows, width = text_grad.shape
    size = rows // CHUNKS

    def body(image_ref, far_ref, text_ref, loss, loss_far, image_out, text_out, loss_out,
             image, far, text, image_sum, text_wide, in_sems, out_sems):
        def chunk(c):
            return pl.ds(pl.multiple_of(c * size, size), size)

        def arrivals(c):
            pairs = ((image_ref, image), (far_ref, far), (text_ref, text))
            return [
                pltpu.make_async_copy(a.at[chunk(c), :], b.at[chunk(c), :], in_sems.at[i, c])
                for i, (a, b) in enumerate(pairs)
            ]

        def departures(c):
            pairs = ((image_sum, image_out), (text_wide, text_out))
            return [
                pltpu.make_async_copy(a.at[chunk(c), :], b.at[chunk(c), :], out_sems.at[i, c])
                for i, (a, b) in enumerate(pairs)
            ]

        def begin(c, _):
            for copy in arrivals(c):
                copy.start()
            return 0

        def work(c, _):
            for copy in arrivals(c):
                copy.wait()
            here = chunk(c)
            image_sum[here, :] = image[here, :] + far[here, :].astype(jnp.float32)
            text_wide[here, :] = text[here, :].astype(jnp.float32)
            for copy in departures(c):
                copy.start()
            return 0

        def end(c, _):
            for copy in departures(c):
                copy.wait()
            return 0

        lax.fori_loop(0, CHUNKS, begin, 0)
        loss_out[...] = (loss[:rows] + loss_far[...]) / count
        lax.fori_loop(0, CHUNKS, work, 0)
        lax.fori_loop(0, CHUNKS, end, 0)

    anywhere, vmem = pl.BlockSpec(memory_space=pl.ANY), pl.BlockSpec(memory_space=pltpu.VMEM)
    wide = jax.ShapeDtypeStruct((rows, width), jnp.float32)
    return pl.pallas_call(
        body,
        in_specs=[anywhere] * 3 + [vmem] * 2,
        out_specs=[anywhere] * 2 + [vmem],
        out_shape=[wide, wide, jax.ShapeDtypeStruct((rows,), jnp.float32)],
        scratch_shapes=[
            pltpu.VMEM((rows, width), jnp.float32),
            pltpu.VMEM((rows, width), jnp.bfloat16),
            pltpu.VMEM((rows, width), jnp.bfloat16),
            pltpu.VMEM((rows, width), jnp.float32),
            pltpu.VMEM((rows, width), jnp.float32),
            pltpu.SemaphoreType.DMA((3, CHUNKS)),
            pltpu.SemaphoreType.DMA((2, CHUNKS)),
        ],
        compiler_params=pltpu.CompilerParams(vmem_limit_bytes=56 * 2**20),
        cost_estimate=pl.CostEstimate(
            flops=rows * width, bytes_accessed=16 * rows * width, transcendentals=0
        ),
    )(image_parts, image_far_part, text_grad, loss_sum, loss_far)


def partner_mask(rnd, width):
    return rnd * width ^ (rnd & 1) * (width // 2)


def solution(mesh):
    groups, width = mesh.shape["dp"], mesh.shape["narrow"]
    count, half = groups * width, width // 2
    over_z = xor_route(count, half)
    over_core = xor_route(count, 1)

    def over_dp(rnd, block):
        return lax.ppermute(block, AXES, xor_route(count, partner_mask(rnd, width)))

    def by_round(step, which, *args):
        branches = [lambda *a, r=r: step(r, *a) for r in range(1, groups)]
        return lax.switch(which, branches, *args)

    def per_device(picture, caption, ids, rnd, scale, shift):
        rnd, scale, shift = rnd[0], scale[0], shift[0]
        rows = picture.shape[0]
        me = lax.axis_index("dp") * width + lax.axis_index("narrow")
        text_at = me ^ partner_mask(rnd, width)
        take = lambda device: lax.dynamic_slice_in_dim(ids, device * rows, rows)
        image_ids = jnp.concatenate([take(me), take(me ^ half)])
        text_ids = jnp.concatenate([take(text_at), take(text_at ^ 1)])

        image_far = lax.ppermute(picture, AXES, over_z)
        text_own = by_round(over_dp, rnd - 1, caption)
        text_near = lax.ppermute(text_own, AXES, over_core)
        images = jnp.concatenate([picture, image_far])
        texts = jnp.concatenate([text_own, text_near])

        logits = scale * dot(images, texts, ((1,), (1,))) + shift
        pair_loss, coef = pair_terms(logits, image_ids, text_ids)
        loss_sum = jnp.sum(pair_loss, axis=1)

        text_parts = lax.optimization_barrier(scale * dot(coef, images, ((0,), (0,))))
        text_far_part = lax.ppermute(text_parts[rows:], AXES, over_core)
        image_parts = lax.optimization_barrier(scale * dot(coef, texts, ((1,), (0,))))
        image_far_part = image_parts[rows:].astype(jnp.bfloat16)
        text_part = (text_parts[:rows] + text_far_part).astype(jnp.bfloat16)

        loss_far = lax.ppermute(loss_sum[rows:], AXES, over_z)
        image_far_part, loss_far = lax.optimization_barrier((image_far_part, loss_far))
        image_far_part = lax.ppermute(image_far_part, AXES, over_z)
        text_grad = by_round(over_dp, rnd - 1, text_part)
        text_grad, image_far_part = lax.optimization_barrier((text_grad, image_far_part))
        return tuple(
            final_call(image_parts, image_far_part, text_grad, loss_sum, loss_far, rows * width)
        )

    in_specs = (P(AXES, None), P(AXES, None), P(), P(), P(), P())
    out_specs = (P(AXES, None), P(AXES, None), P(AXES))
    return jax.shard_map(
        per_device, mesh=mesh, in_specs=in_specs, out_specs=out_specs, check_vma=False
    )
```

```python
import jax
import jax.numpy as jnp
from jax import lax
from jax.sharding import PartitionSpec as P

AXES = ("dp", "narrow")


def xor_route(count, mask):
    return [(d, d ^ mask) for d in range(count)]


def pair_terms(logits, left_ids, right_ids):
    same = left_ids[:, None] == right_ids[None, :]
    z = jnp.where(same, logits, -logits)
    tail = jnp.exp(-jnp.abs(z))
    pair_loss = jnp.maximum(-z, 0.0) + jnp.log1p(tail)
    share = jnp.where(z > 0, tail, 1.0) / (1.0 + tail)
    coef = jnp.where(same, -share, share).astype(jnp.bfloat16)
    return pair_loss, coef


def dot(a, b, dims):
    return lax.dot_general(a, b, (dims, ((), ())), preferred_element_type=jnp.float32)


def partner_mask(rnd, width):
    return rnd * width ^ (rnd & 1) * (width // 2)


def solution(mesh):
    groups, width = mesh.shape["dp"], mesh.shape["narrow"]
    count, half = groups * width, width // 2
    over_z = xor_route(count, half)
    over_core = xor_route(count, 1)

    def over_dp(rnd, block):
        return lax.ppermute(block, AXES, xor_route(count, partner_mask(rnd, width)))

    def by_round(step, which, *args):
        branches = [lambda *a, r=r: step(r, *a) for r in range(1, groups)]
        return lax.switch(which, branches, *args)

    def per_device(picture, caption, ids, rnd, scale, shift):
        rnd, scale, shift = rnd[0], scale[0], shift[0]
        rows = picture.shape[0]
        me = lax.axis_index("dp") * width + lax.axis_index("narrow")
        text_at = me ^ partner_mask(rnd, width)
        take = lambda device: lax.dynamic_slice_in_dim(ids, device * rows, rows)
        image_ids = jnp.concatenate([take(me), take(me ^ half)])
        text_ids = jnp.concatenate([take(text_at), take(text_at ^ 1)])

        image_far = lax.ppermute(picture, AXES, over_z)
        text_own = by_round(over_dp, rnd - 1, caption)
        text_near = lax.ppermute(text_own, AXES, over_core)
        images = jnp.concatenate([picture, image_far])
        texts = jnp.concatenate([text_own, text_near])

        logits = scale * dot(images, texts, ((1,), (1,))) + shift
        pair_loss, coef = pair_terms(logits, image_ids, text_ids)
        loss_sum = jnp.sum(pair_loss, axis=1)

        text_parts = lax.optimization_barrier(scale * dot(coef, images, ((0,), (0,))))
        text_far_part = lax.ppermute(text_parts[rows:], AXES, over_core)
        image_far_part = (scale * dot(coef[rows:], texts, ((1,), (0,)))).astype(jnp.bfloat16)
        text_part = (text_parts[:rows] + text_far_part).astype(jnp.bfloat16)

        loss_far = lax.ppermute(loss_sum[rows:], AXES, over_z)
        image_far_part, loss_far = lax.optimization_barrier((image_far_part, loss_far))
        image_far_part = lax.ppermute(image_far_part, AXES, over_z)
        text_grad = by_round(over_dp, rnd - 1, text_part)
        text_grad, image_far_part = lax.optimization_barrier((text_grad, image_far_part))
        image_grad = scale * dot(coef[:rows], texts, ((1,), (0,))) + image_far_part.astype(jnp.float32)
        row_loss = (loss_sum[:rows] + loss_far) / (rows * width)
        return image_grad, text_grad.astype(jnp.float32), row_loss

    in_specs = (P(AXES, None), P(AXES, None), P(), P(), P(), P())
    out_specs = (P(AXES, None), P(AXES, None), P(AXES))
    return jax.shard_map(
        per_device, mesh=mesh, in_specs=in_specs, out_specs=out_specs, check_vma=False
    )
```

```python
import jax
import jax.numpy as jnp
from jax import lax
from jax.sharding import PartitionSpec as P

AXES = ("dp", "narrow")


def xor_route(count, mask):
    return [(d, d ^ mask) for d in range(count)]


def pair_terms(logits, left_ids, right_ids):
    same = left_ids[:, None] == right_ids[None, :]
    z = jnp.where(same, logits, -logits)
    tail = jnp.exp(-jnp.abs(z))
    pair_loss = jnp.maximum(-z, 0.0) + jnp.log1p(tail)
    share = jnp.where(z > 0, tail, 1.0) / (1.0 + tail)
    coef = jnp.where(same, -share, share).astype(jnp.bfloat16)
    return pair_loss, coef


def dot(a, b, dims):
    return lax.dot_general(a, b, (dims, ((), ())), preferred_element_type=jnp.float32)


def partner_mask(rnd, width):
    return rnd * width ^ (rnd & 1) * (width // 2)


def solution(mesh):
    groups, width = mesh.shape["dp"], mesh.shape["narrow"]
    count, half = groups * width, width // 2
    over_z = xor_route(count, half)
    over_core = xor_route(count, 1)

    def over_dp(rnd, block):
        return lax.ppermute(block, AXES, xor_route(count, partner_mask(rnd, width)))

    def by_round(step, which, *args):
        branches = [lambda *a, r=r: step(r, *a) for r in range(1, groups)]
        return lax.switch(which, branches, *args)

    def per_device(picture, caption, ids, rnd, scale, shift):
        rnd, scale, shift = rnd[0], scale[0], shift[0]
        rows = picture.shape[0]
        me = lax.axis_index("dp") * width + lax.axis_index("narrow")
        text_at = me ^ partner_mask(rnd, width)
        take = lambda device: lax.dynamic_slice_in_dim(ids, device * rows, rows)
        image_ids = jnp.concatenate([take(me), take(me ^ half)])
        own_ids, near_ids = take(text_at), take(text_at ^ 1)

        image_far = lax.ppermute(picture, AXES, over_z)
        text_own = by_round(over_dp, rnd - 1, caption)
        text_near = lax.ppermute(text_own, AXES, over_core)
        images = jnp.concatenate([picture, image_far])

        def pairs(text, text_ids):
            logits = scale * dot(images, text, ((1,), (1,))) + shift
            pair_loss, coef = pair_terms(logits, image_ids, text_ids)
            return jnp.sum(pair_loss, axis=1), coef

        def image_part(mine):
            return scale * (
                dot(own_coef[mine], text_own, ((1,), (0,))) + dot(near_coef[mine], text_near, ((1,), (0,)))
            )

        own_loss, own_coef = pairs(text_own, own_ids)
        text_near, own_coef = lax.optimization_barrier((text_near, own_coef))
        near_loss, near_coef = pairs(text_near, near_ids)
        loss_sum = own_loss + near_loss

        text_far_part = scale * dot(near_coef, images, ((0,), (0,)))
        text_far_part = lax.ppermute(text_far_part, AXES, over_core)
        image_far_part = image_part(slice(rows, None)).astype(jnp.bfloat16)
        text_part = scale * dot(own_coef, images, ((0,), (0,)))
        text_part = (text_part + text_far_part).astype(jnp.bfloat16)

        loss_far = lax.ppermute(loss_sum[rows:], AXES, over_z)
        image_far_part, loss_far = lax.optimization_barrier((image_far_part, loss_far))
        image_far_part = lax.ppermute(image_far_part, AXES, over_z)
        text_grad = by_round(over_dp, rnd - 1, text_part)
        text_grad, image_far_part = lax.optimization_barrier((text_grad, image_far_part))
        image_grad = image_part(slice(rows)) + image_far_part.astype(jnp.float32)
        row_loss = (loss_sum[:rows] + loss_far) / (rows * width)
        return image_grad, text_grad.astype(jnp.float32), row_loss

    in_specs = (P(AXES, None), P(AXES, None), P(), P(), P(), P())
    out_specs = (P(AXES, None), P(AXES, None), P(AXES))
    return jax.shard_map(
        per_device, mesh=mesh, in_specs=in_specs, out_specs=out_specs, check_vma=False
    )
```

```python
import jax
import jax.numpy as jnp
from jax import lax
from jax.sharding import PartitionSpec as P

AXES = ("dp", "narrow")


def xor_route(count, mask):
    return [(d, d ^ mask) for d in range(count)]


def pair_terms(logits, left_ids, right_ids):
    same = left_ids[:, None] == right_ids[None, :]
    z = jnp.where(same, logits, -logits)
    tail = jnp.exp(-jnp.abs(z))
    pair_loss = jnp.maximum(-z, 0.0) + jnp.log1p(tail)
    share = jnp.where(z > 0, tail, 1.0) / (1.0 + tail)
    coef = jnp.where(same, -share, share).astype(jnp.bfloat16)
    return pair_loss, coef


def dot(a, b, dims):
    return lax.dot_general(a, b, (dims, ((), ())), preferred_element_type=jnp.float32)


def partner_mask(rnd, width):
    return rnd * width ^ (rnd & 1) * (width // 2)


def solution(mesh):
    groups, width = mesh.shape["dp"], mesh.shape["narrow"]
    count, half = groups * width, width // 2
    over_z = xor_route(count, half)
    over_core = xor_route(count, 1)

    def over_dp(rnd, block):
        return lax.ppermute(block, AXES, xor_route(count, partner_mask(rnd, width)))

    def by_round(step, which, *args):
        branches = [lambda *a, r=r: step(r, *a) for r in range(1, groups)]
        return lax.switch(which, branches, *args)

    def per_device(picture, caption, ids, rnd, scale, shift):
        rnd, scale, shift = rnd[0], scale[0], shift[0]
        rows = picture.shape[0]
        me = lax.axis_index("dp") * width + lax.axis_index("narrow")
        text_at = me ^ partner_mask(rnd, width)
        take = lambda device: lax.dynamic_slice_in_dim(ids, device * rows, rows)
        image_ids = jnp.concatenate([take(me), take(me ^ half)])
        text_ids = jnp.concatenate([take(text_at), take(text_at ^ 1)])

        image_far = lax.ppermute(picture, AXES, over_z)
        text_own = by_round(over_dp, rnd - 1, caption)
        text_near = lax.ppermute(text_own, AXES, over_core)
        images = jnp.concatenate([picture, image_far])
        texts = jnp.concatenate([text_own, text_near])

        logits = scale * dot(images, texts, ((1,), (1,))) + shift
        pair_loss, coef = pair_terms(logits, image_ids, text_ids)
        loss_sum = jnp.sum(pair_loss, axis=1)
        text_own, text_near, coef = lax.optimization_barrier((text_own, text_near, coef))
        texts = lax.optimization_barrier(jnp.concatenate([text_own, text_near]))

        text_parts = lax.optimization_barrier(scale * dot(coef, images, ((0,), (0,))))
        text_far_part = lax.ppermute(text_parts[rows:], AXES, over_core)
        image_far_part = (scale * dot(coef[rows:], texts, ((1,), (0,)))).astype(jnp.bfloat16)
        text_part = (text_parts[:rows] + text_far_part).astype(jnp.bfloat16)

        loss_far = lax.ppermute(loss_sum[rows:], AXES, over_z)
        image_far_part, loss_far = lax.optimization_barrier((image_far_part, loss_far))
        image_far_part = lax.ppermute(image_far_part, AXES, over_z)
        text_grad = by_round(over_dp, rnd - 1, text_part)
        text_grad, image_far_part = lax.optimization_barrier((text_grad, image_far_part))
        image_grad = scale * dot(coef[:rows], texts, ((1,), (0,))) + image_far_part.astype(jnp.float32)
        row_loss = (loss_sum[:rows] + loss_far) / (rows * width)
        return image_grad, text_grad.astype(jnp.float32), row_loss

    in_specs = (P(AXES, None), P(AXES, None), P(), P(), P(), P())
    out_specs = (P(AXES, None), P(AXES, None), P(AXES))
    return jax.shard_map(
        per_device, mesh=mesh, in_specs=in_specs, out_specs=out_specs, check_vma=False
    )
```
